128 devices in a mesh: expert: 64 (over y, z, x), wshard: 2 (over core).
Axes of the slice: x: 4, y: 4, z: 4, core: 2. Of those that a mesh axis runs over, the one named last changes fastest.
Arguments:
- tokens: bfloat16 [32768, 768], P(('expert', 'wshard')), may hold values from -6 to 6
- lengths: int32 [128, 4], P(('expert', 'wshard')), may hold values from 1 to 128, 256 in all within a row
- routes: int32 [32768, 2], P(('expert', 'wshard')), may hold values from 0 to 63, all different within a row; in each aligned block of 256 rows (0 to 255, 256 to 511, ...) at most 12 rows name the same one
- w_query: bfloat16 [768, 768], P('wshard'), may hold values from -0.21875 to 0.21875
- w_key: bfloat16 [768, 768], P('wshard'), may hold values from -0.21875 to 0.21875
- w_value: bfloat16 [768, 768], P('wshard'), may hold values from -0.21875 to 0.21875
- w_output: bfloat16 [768, 768], P('wshard'), may hold values from -0.625 to 0.625
- w_router: bfloat16 [768, 64], P('wshard'), may hold values from -0.21875 to 0.21875
- bias_table: bfloat16 [32, 12], P('wshard'), may hold values from -4 to 4
- attn_gain: bfloat16 [768], P('wshard'), may hold values from 0.5 to 1.5
- moe_gain: bfloat16 [768], P('wshard'), may hold values from 0.5 to 1.5
- expert_up: bfloat16 [64, 768, 3072], P('expert', None, 'wshard'), may hold values from -0.21875 to 0.21875
- expert_down: bfloat16 [64, 3072, 768], P('expert', 'wshard'), may hold values from -0.109375 to 0.109375
- cotangent: bfloat16 [32768, 768], P(('expert', 'wshard')), may hold values from -6 to 6
Outputs:
- layer_out: bfloat16 [32768, 768], P(('expert', 'wshard'))
- grad_tokens: bfloat16 [32768, 768], P(('expert', 'wshard'))
- grad_query: float32 [768, 768], P('wshard')
- grad_key: float32 [768, 768], P('wshard')
- grad_value: float32 [768, 768], P('wshard')
- grad_output: float32 [768, 768], P('wshard')
- grad_router: float32 [768, 64], P('wshard')
- grad_table: float32 [32, 12], P('wshard')
- grad_attngain: float32 [768], P('wshard')
- grad_moegain: float32 [768], P('wshard')
- grad_up: float32 [64, 768, 3072], P('expert', None, 'wshard')
- grad_down: float32 [64, 3072, 768], P('expert', 'wshard')
The draws below stay inside these ranges and needn't reach their ends.
Inputs may be any that keep to these rules, and one draw needn't show every extreme that they name: Each device's 4 lengths sum to 256; the longest is 128 on every device. `routes`: the two experts of a token differ; among the tokens of one device each expert is named by at most 12 tokens, and by exactly 12 for some expert.
All inputs are finite; a program needn't handle non-finite values.
Results may differ from the reference program's by a relative error of at most 0.015.
Values may be sent and summed in bfloat16 or wider, within the bound.
No kernel may reach another device: no remote copies, remote signals or barrier semaphores. Data moves between devices by JAX's collectives and lax.ppermute only.
A program may use at most 128 MiB of HBM per device.

```python
import math
from functools import partial
import jax
import jax.numpy as jnp
import numpy as np
from jax import lax

D = 768
H = 12
HD = 64
FF = 3072
NB = 32
SEQ_DEV = 4
TOK_DEV = 256
EXPERTS = 64
CAP = 12
TOKENS = 32768
DEVICES = 128


def level_of(own_key, extent, shards, least, largest):
    gain, own = 1.0, jax.random.fold_in(own_key, 6)
    for dim, blocks in shards:
        heights = jnp.exp(jax.random.uniform(jax.random.fold_in(own, dim), (blocks,), jnp.float32, least / len(shards), largest / len(shards)))
        gain = gain * jnp.repeat(heights, extent[dim] // blocks).reshape([-1 if axis == dim else 1 for axis in range(len(extent))])
    return gain


def length_profile(amount, total, most, slope):
    weights = [(1 << 20) // math.isqrt(standing ** slope) + 1 for standing in range(2, amount + 1)]
    surplus, holding = total - most - (amount - 1), [1] * (amount - 1)
    while surplus > 0:
        candidates = [i for i in range(amount - 1) if holding[i] < most]
        pool, left = sum([weights[i] for i in candidates]), surplus
        for i in candidates:
            addition = min(most - holding[i], max(1, left * weights[i] // pool), surplus)
            holding[i] = holding[i] + addition
            surplus = surplus - addition
    return np.array([most] + holding)


def uneven(own_key, amount, total, limit, lean):
    if amount == 2:
        one = jax.random.randint(own_key, (), max(1, total - limit), min(limit, total - 1) + 1)
        return jnp.stack([one, total - one])
    sizes = jnp.asarray(length_profile(amount, total, limit, lean), jnp.int32)
    couples = (amount - 1) // 2
    donor, sink = sizes[1:1 + 2 * couples:2], sizes[2:2 + 2 * couples:2]
    margin = jnp.minimum(donor - 1, limit - sink)
    passed = jax.random.randint(jax.random.fold_in(own_key, 1), (couples,), 0, 1 << 20) % (margin + 1)
    sizes = sizes.at[1:1 + 2 * couples:2].set(donor - passed).at[2:2 + 2 * couples:2].set(sink + passed)
    return sizes[jax.random.permutation(jax.random.fold_in(own_key, 2), amount)]


def assign_block(stream_key, own, number, rows, count, top, bound, skew):
    order = jax.random.permutation(stream_key, count)
    heavy_load, common = shares(count, rows * top, bound, skew, True), shares(count, rows * top, bound, skew, False)
    places = jnp.arange(count)

    def named(tallies, rotation):
        used = int((tallies > 0).sum())
        fixed = max(1, used // 4)
        shifted = fixed + (places - fixed + rotation * (used - fixed)) % max(1, count - fixed)
        return jnp.zeros((count,), jnp.int32).at[order[jnp.where(places < fixed, places, shifted)]].set(jnp.asarray(tallies, jnp.int32))

    tallies = jnp.where(number % 4 == 0, named(heavy_load, number // 4), named(common, number - number // 4 - 1))
    mixed = jax.random.permutation(jax.random.fold_in(own, 3), count)
    donor, sink = mixed[0:count // 2 * 2:2], mixed[1:count // 2 * 2:2]
    room = jnp.minimum(tallies[donor] - 1, bound - tallies[sink]) // 2
    room = jnp.where((donor == order[0]) | (sink == order[0]) | (tallies[sink] == 0), 0, jnp.maximum(room, 0))
    shifted = jax.random.randint(jax.random.fold_in(own, 4), (count // 2,), 0, 1 << 20) % (room + 1)
    tallies = tallies.at[donor].add(-shifted).at[sink].add(shifted)
    labels = jnp.searchsorted(jnp.cumsum(tallies), jnp.arange(rows * top), side="right").astype(jnp.int32)
    table = labels.reshape(top, rows).T
    table = table[jax.random.permutation(jax.random.fold_in(own, 1), rows)]
    rotation = jax.random.randint(jax.random.fold_in(own, 2), (rows, 1), 0, top)
    return jnp.take_along_axis(table, (jnp.arange(top)[None, :] + rotation) % top, axis=1)


def shares(count, total, bound, skew, full):
    weights = [(1 << 20) // math.isqrt(standing ** skew) + 1 for standing in range(1, count + 1)]
    largest = bound if full else min(bound, max(-(-total // count), total * weights[0] // sum(weights)))
    least = 1 if total - largest >= count - 1 else 0
    counts, surplus = [largest] + [least] * (count - 1), total - largest - least * (count - 1)
    while surplus > 0:
        movable = [i for i in range(1, count) if counts[i] < largest] or [i for i in range(1, count) if counts[i] < bound]
        mass, budget = sum([weights[i] for i in movable]), surplus
        for i in movable:
            more = min(bound - counts[i], max(1, budget * weights[i] // mass), surplus)
            counts[i] = counts[i] + more
            surplus = surplus - more
    return np.array(counts)


def scatter_about(key, shape, spread, reach, cuts=(), kind=jnp.bfloat16):
    values = jax.random.normal(key, shape, jnp.float32) * spread
    if len(cuts) > 0:
        values = level_of(key, shape, cuts, -0.22, 0.18) * values
    return jnp.clip(values, min=-reach, max=reach).astype(kind)


def setup_inputs(seed: int = 0) -> dict:
    key_list = jax.random.split(jax.random.key(seed), 15)
    tokens = scatter_about(key_list[0], (TOKENS, D), 1.0, 6.0, ((0, 128),))
    lengths = jax.vmap(lambda own: uneven(own, SEQ_DEV, TOK_DEV, TOK_DEV // 2, 2))(jax.random.split(key_list[1], DEVICES)).reshape((DEVICES, SEQ_DEV)).astype(jnp.int32)
    routes_keys = jax.random.split(jax.random.fold_in(key_list[2], 1), TOKENS // TOK_DEV)
    routes_turns = jax.random.permutation(jax.random.fold_in(key_list[2], 3), TOKENS // TOK_DEV)
    routes = jax.vmap(lambda own, number: assign_block(jax.random.fold_in(key_list[2], 2), own, number, TOK_DEV, EXPERTS, 2, CAP, 2))(routes_keys, routes_turns).reshape((TOKENS, 2))
    w_query = scatter_about(key_list[3], (D, D), D ** -0.5, 0.21875, ((0, 2),))
    w_key = scatter_about(key_list[4], (D, D), D ** -0.5, 0.21875, ((0, 2),))
    w_value = scatter_about(key_list[5], (D, D), D ** -0.5, 0.21875, ((0, 2),))
    w_output = scatter_about(key_list[6], (D, D), (D // 8) ** -0.5, 0.625, ((0, 2),))
    w_router = scatter_about(key_list[7], (D, EXPERTS), D ** -0.5, 0.21875, ((0, 2),))
    bias_table = scatter_about(key_list[8], (NB, H), 1.0, 4.0, ((0, 2),))
    attn_gain = jnp.clip(1.0 + 0.1 * jax.random.normal(key_list[9], (D,), jnp.float32), 0.5, 1.5).astype(jnp.bfloat16)
    moe_gain = jnp.clip(1.0 + 0.1 * jax.random.normal(key_list[10], (D,), jnp.float32), 0.5, 1.5).astype(jnp.bfloat16)
    expert_up = scatter_about(key_list[11], (EXPERTS, D, FF), D ** -0.5, 0.21875, ((0, 64), (2, 2)))
    expert_down = scatter_about(key_list[12], (EXPERTS, FF, D), FF ** -0.5, 0.109375, ((0, 64), (1, 2)))
    cotangent = scatter_about(key_list[13], (TOKENS, D), 1.0, 6.0, ((0, 128),))
    return dict(tokens=tokens, lengths=lengths, routes=routes, w_query=w_query, w_key=w_key, w_value=w_value, w_output=w_output, w_router=w_router, bias_table=bias_table, attn_gain=attn_gain, moe_gain=moe_gain, expert_up=expert_up, expert_down=expert_down, cotangent=cotangent)


@jax.custom_vjp
def low(v):
    return lax.optimization_barrier(v.astype(jnp.bfloat16)).astype(jnp.float32)

@jax.custom_vjp
def low_back(v):
    return v

def low_keep(v):
    return (low(v), None)

def low_pass(kept, grad):
    return (grad,)

def back_keep(v):
    return (v, None)

def back_low(kept, grad):
    return (low(grad),)
low.defvjp(low_keep, low_pass)
low_back.defvjp(back_keep, back_low)
exact_span = 16
far_span = 128
neg_fill = -1000000000.0
epsilon = 1e-06
highest = lax.Precision.HIGHEST

def rounded(activation):
    return low_back(low(activation))

def bucket_matrix(row_count):
    thresholds = np.array([int(exact_span * (far_span / exact_span) ** (position / (NB - exact_span))) for position in range(1, NB - exact_span)], np.int32)
    row_ids = jnp.arange(row_count, dtype=jnp.int32)
    distance = jnp.maximum(row_ids[:, None] - row_ids[None, :], 0)
    beyond = lax.optimization_barrier(jnp.sum((distance[:, :, None] >= jnp.asarray(thresholds)[None, None, :]).astype(jnp.int32), axis=2))
    return jnp.where(distance < exact_span, distance, exact_span + beyond)

def segment_mask(length_row, row_count):
    boundary = jnp.cumsum(length_row).astype(jnp.int32)
    row_ids = jnp.arange(row_count, dtype=jnp.int32)
    segment = lax.optimization_barrier(jnp.sum((row_ids[:, None] >= boundary[None, :]).astype(jnp.int32), axis=1))
    return (segment[:, None] == segment[None, :]) & (row_ids[None, :] <= row_ids[:, None])

def route_slots(routes_dev, experts_total):
    chosen = (routes_dev[:, :, None] == jnp.arange(experts_total, dtype=jnp.int32)[None, None, :]).astype(jnp.int32)
    flattened = chosen.reshape(-1, experts_total)
    before = jnp.cumsum(flattened, axis=0) - flattened
    return lax.optimization_barrier(jnp.sum(before * flattened, axis=1)).reshape(routes_dev.shape).astype(jnp.int32)

def norm_scaled(activation, gain_vector):
    inverse = lax.rsqrt(lax.optimization_barrier(jnp.mean(activation * activation, axis=-1, keepdims=True)) + epsilon)
    return activation * inverse * gain_vector

def forward(tokens, w_query, w_key, w_value, w_output, w_router, bias_table, attn_gain, moe_gain, expert_up, expert_down, lengths, routes):
    attn_in = low(norm_scaled(tokens, attn_gain))
    queries = rounded(jnp.dot(attn_in, w_query, precision=highest))
    key_rows = rounded(jnp.dot(attn_in, w_key, precision=highest))
    value_rows = rounded(jnp.dot(attn_in, w_value, precision=highest))
    score_bias = jnp.transpose(bias_table[bucket_matrix(TOK_DEV)], (2, 0, 1))
    score_scale = HD ** (-0.5)

    def attend(operands):
        query_block, key_block, value_block, length_row = operands
        allowed = segment_mask(length_row, TOK_DEV)
        query_heads = query_block.reshape(TOK_DEV, H, HD)
        key_heads = key_block.reshape(TOK_DEV, H, HD)
        value_heads = value_block.reshape(TOK_DEV, H, HD)
        scores = jnp.einsum('qhd,khd->hqk', query_heads, key_heads, precision=highest) * score_scale + score_bias
        scores = low_back(jnp.where(allowed[None], scores, neg_fill))
        attn_probs = jax.nn.softmax(scores, axis=-1)
        mixed_heads = jnp.einsum('hqk,khd->qhd', low(attn_probs), value_heads, precision=highest)
        return rounded(mixed_heads.reshape(TOK_DEV, D))
    attn_out = lax.map(jax.checkpoint(attend), (queries.reshape(DEVICES, TOK_DEV, D), key_rows.reshape(DEVICES, TOK_DEV, D), value_rows.reshape(DEVICES, TOK_DEV, D), lengths)).reshape(TOKENS, D)
    residual = tokens + low_back(jnp.dot(attn_out, w_output, precision=highest))
    moe_in = low(norm_scaled(residual, moe_gain))
    logits = low_back(jnp.dot(moe_in, w_router, precision=highest))
    gate_pair = jax.nn.softmax(jnp.take_along_axis(logits, routes, axis=1), axis=-1)
    slot_ids = jax.vmap(partial(route_slots, experts_total=EXPERTS))(routes.reshape(DEVICES, TOK_DEV, 2)).reshape(TOKENS, 2)
    device_ids = jnp.repeat(jnp.arange(DEVICES, dtype=jnp.int32), TOK_DEV)[:, None]
    column = (device_ids * CAP + slot_ids).astype(jnp.int32)
    buffer = jnp.zeros((EXPERTS, DEVICES * CAP, D), tokens.dtype)
    buffer = buffer.at[routes, column].add(jnp.broadcast_to(moe_in[:, None, :], (TOKENS, 2, D)))
    buffer = low_back(buffer)

    def expert_apply(operands):
        row_block, first_matrix, second_matrix = operands
        hidden = low_back(jnp.dot(row_block, first_matrix, precision=highest))
        active = low(jax.nn.gelu(hidden, approximate=True))
        return rounded(jnp.dot(active, second_matrix, precision=highest))
    results = lax.map(jax.checkpoint(expert_apply), (buffer, expert_up, expert_down))
    picked = results[routes, column]
    return residual + lax.optimization_barrier(jnp.sum(gate_pair[:, :, None] * picked, axis=1))

def reference(tokens, lengths, routes, w_query, w_key, w_value, w_output, w_router, bias_table, attn_gain, moe_gain, expert_up, expert_down, cotangent):
    floats = tuple((operand.astype(jnp.float32) for operand in (tokens, w_query, w_key, w_value, w_output, w_router, bias_table, attn_gain, moe_gain, expert_up, expert_down)))

    def apply_layer(*operands):
        return forward(*operands, lengths, routes)
    layer_out, pullback = jax.vjp(apply_layer, *floats)
    gradients = pullback(cotangent.astype(jnp.float32))
    return (layer_out.astype(jnp.bfloat16), gradients[0].astype(jnp.bfloat16), gradients[1], gradients[2], gradients[3], gradients[4], gradients[5], gradients[6], gradients[7], gradients[8], gradients[9], gradients[10])
```

```python
from functools import partial

import jax
import jax.numpy as jnp
import numpy as np
from jax import lax
from jax.experimental import pallas as pl
from jax.experimental.pallas import tpu as pltpu
from jax.sharding import PartitionSpec as P

ROWS = 256
WIDTH = 768
HALF = 384
HEADS = 12
HEAD = 64
NB = 32
CAP = 12
EXPERTS = 64
SLOTS = EXPERTS * 2 * CAP
FFH = 1536
LANES = 128
TABLE_LANE = 64
GAIN_ROW = 384
EXTRA = 4 * HALF * WIDTH // LANES
DENSE = EXPERTS * 152
SCALE = HEAD ** (-0.5)
NEG = -1000000000.0
EPS = 1e-06
FORWARD_LIMIT = 32 * 1024 * 1024
EXPERT_LIMIT = 26 * 1024 * 1024
GRAD_LIMIT = 16 * 1024 * 1024
BACKWARD_LIMIT = 36 * 1024 * 1024

bfloat = jnp.bfloat16
single = jnp.float32
THRESHOLDS = [int(16 * 8.0 ** (j / 16)) for j in range(1, 16)]

ROWS_ROWS = (((1,), (1,)), ((), ()))
COLS_COLS = (((0,), (0,)), ((), ()))


def dot(a, b):
    return jnp.dot(a, b, preferred_element_type=single)


def dot_nt(a, b):
    return lax.dot_general(a, b, ROWS_ROWS, preferred_element_type=single)


def dot_tn(a, b):
    return lax.dot_general(a, b, COLS_COLS, preferred_element_type=single)


def iota(shape, dim):
    return lax.broadcasted_iota(jnp.int32, shape, dim)


def bucket_of(distance):
    beyond = jnp.zeros_like(distance)
    for threshold in THRESHOLDS:
        beyond = beyond + (distance >= threshold).astype(jnp.int32)
    return jnp.where(distance < 16, distance, 16 + beyond)


def in_order(core, mine, theirs, axis):
    return jnp.where(
        core == 0,
        jnp.concatenate([mine, theirs], axis=axis),
        jnp.concatenate([theirs, mine], axis=axis),
    )


def gain_rows(core, pack_mine, pack_theirs):
    gains = []
    mine = pack_mine[GAIN_ROW : GAIN_ROW + 16, :].astype(single)
    theirs = pack_theirs[GAIN_ROW : GAIN_ROW + 16, :].astype(single)
    for first in (0, 3):
        rows = [
            jnp.concatenate([block[first + i : first + i + 1] for i in range(3)], axis=1)
            for block in (mine, theirs)
        ]
        gains.append(in_order(core, rows[0], rows[1], 1))
    return gains


def unit_rows(value):
    inverse = lax.rsqrt(jnp.mean(value * value, axis=-1, keepdims=True) + EPS)
    return value * inverse, inverse


def pair_of(h):
    return slice((h // 2) * 2 * HEAD, (h // 2 + 1) * 2 * HEAD)


def head_sides():
    lane = iota((1, 2 * HEAD), 1)
    first = (lane < HEAD).astype(single)
    return (first.astype(bfloat), (1.0 - first).astype(bfloat)), lane < HEAD


def start_all(pairs, sems, first=0):
    copies = [
        pltpu.make_async_copy(src, dst, sems.at[first + i]) for i, (src, dst) in enumerate(pairs)
    ]
    for copy in copies:
        copy.start()
    return copies


def forward_kernel(
    core_ref,
    len_ref,
    routes_ref,
    x_hbm,
    cot_hbm,
    wq_mh,
    wk_mh,
    wv_mh,
    wo_mh,
    up_hbm,
    down_hbm,
    wq_t,
    wk_t,
    wv_t,
    wo_t,
    pack_m,
    pack_t,
    send_ref,
    meta_ref,
    up_near,
    down_near,
    q_hbm,
    k_hbm,
    v_hbm,
    out_hbm,
    res_hbm,
    low_hbm,
    probs_hbm,
    wq_th,
    wk_th,
    wv_th,
    wo_th,
    x_ref,
    cot_ref,
    wq_m,
    wk_m,
    wv_m,
    wo_m,
    q_ref,
    k_ref,
    v_ref,
    out_ref,
    res_ref,
    low_ref,
    probs_ref,
    stack,
    in_sems,
    out_sems,
):
    arriving = start_all(
        [
            (x_hbm, x_ref),
            (wq_mh, wq_m),
            (wk_mh, wk_m),
            (wv_mh, wv_m),
            (wo_mh, wo_m),
            (cot_hbm, cot_ref),
        ],
        in_sems,
    )
    core = core_ref[0]
    mine = pl.ds(pl.multiple_of(core * HALF, HALF), HALF)
    theirs = pl.ds(pl.multiple_of((1 - core) * HALF, HALF), HALF)
    gain_attn, gain_moe = gain_rows(core, pack_m, pack_t)
    row, col = iota((ROWS, ROWS), 0), iota((ROWS, ROWS), 1)
    seg_row, seg_col = jnp.zeros_like(row), jnp.zeros_like(col)
    edge = 0
    for i in range(4):
        edge = edge + len_ref[0, i]
        seg_row = seg_row + (row >= edge).astype(jnp.int32)
        seg_col = seg_col + (col >= edge).astype(jnp.int32)
    allowed = (seg_row == seg_col) & (col <= row)
    distance = (ROWS - iota((NB, ROWS), 1)) % ROWS
    hot = (bucket_of(distance) == iota((NB, ROWS), 0)).astype(single).astype(bfloat)
    table = in_order(core, pack_m[0:16, :].astype(single), pack_t[0:16, :].astype(single), 0)
    by_distance = dot_tn(table.astype(bfloat), hot)

    lane = iota((ROWS, LANES), 1)
    chosen = [(lane == routes_ref[:, j : j + 1]).astype(single) for j in range(2)]
    earlier = (col < row).astype(single).astype(bfloat)
    before = dot(earlier, (chosen[0] + chosen[1]).astype(bfloat))
    places = []
    for j in range(2):
        slot = jnp.sum(before * chosen[j], axis=1, keepdims=True)
        places.append(routes_ref[:, j : j + 1].astype(single) * (2 * CAP) + slot)
    arriving[0].wait()
    x = x_ref[...].astype(single)
    low_ref[...] = (unit_rows(x)[0] * gain_attn).astype(bfloat)
    own, other = low_ref[:, mine], low_ref[:, theirs]
    for i, (ref, w_m, w_t) in enumerate(
        ((q_ref, wq_m, wq_t), (k_ref, wk_m, wk_t), (v_ref, wv_m, wv_t))
    ):
        arriving[1 + i].wait()
        ref[...] = (dot(own, w_m[...]) + dot(other, w_t[...])).astype(bfloat)
    arriving += start_all([(up_hbm, up_near), (down_hbm, down_near)], in_sems, 6)
    leaving = start_all([(q_ref, q_hbm), (k_ref, k_hbm), (v_ref, v_hbm)], out_sems)
    leaving += start_all(
        [(wq_t, wq_th), (wk_t, wk_th), (wv_t, wv_th), (wo_t, wo_th)], out_sems, 7
    )

    sides, first_side = head_sides()

    def raw_scores(h):
        pair = pair_of(h)
        return dot_nt(q_ref[:, pair] * sides[h % 2], k_ref[:, pair])

    def finish(h):
        pair = pair_of(h)
        values = v_ref[:, pair]
        mixed = jnp.where(first_side, dot(probs_ref[h], values), dot(probs_ref[h + 1], values))
        out_ref[:, pair] = mixed.astype(bfloat)

    ahead = raw_scores(0)
    for h in range(HEADS):
        raw = ahead
        if h + 1 < HEADS:
            ahead = raw_scores(h + 1)
        line = by_distance[TABLE_LANE + h : TABLE_LANE + h + 1, :]
        bias = pltpu.roll(
            jnp.broadcast_to(line, (ROWS, ROWS)), 0, 1, stride=1, stride_axis=0
        )
        scores = jnp.where(allowed, raw * SCALE + bias, NEG)
        exponent = jnp.exp(scores - jnp.max(scores, axis=1, keepdims=True))
        low = (exponent * (1.0 / jnp.sum(exponent, axis=1, keepdims=True))).astype(bfloat)
        probs_ref[h] = low
        if h % 2 == 1 and h > 1:
            finish(h - 3)
    finish(HEADS - 2)

    leaving += start_all([(probs_ref, probs_hbm), (out_ref, out_hbm)], out_sems, 3)
    for copy in arriving[4:6]:
        copy.wait()
    residual = x + dot(out_ref[:, mine], wo_m[...]) + dot(out_ref[:, theirs], wo_t[...])
    res_ref[...] = residual
    moe_in = (unit_rows(residual)[0] * gain_moe).astype(bfloat)
    low_ref[...] = moe_in
    leaving += start_all([(res_ref, res_hbm), (low_ref, low_hbm)], out_sems, 5)
    logits = dot(low_ref[:, mine], pack_m[0:HALF, :]) + dot(
        low_ref[:, theirs], pack_t[0:HALF, :]
    )
    pair_logits = []
    for j in range(2):
        pair_logits.append(
            jnp.sum(jnp.where(chosen[j] > 0, logits, 0.0), axis=1, keepdims=True)
        )
    peak = jnp.maximum(pair_logits[0], pair_logits[1])
    powers = [jnp.exp(value - peak) for value in pair_logits]
    gates = [power / (powers[0] + powers[1]) for power in powers]
    meta = jnp.zeros((ROWS, LANES), single)
    for i, column in enumerate(places + gates):
        meta = jnp.where(lane == i, column, meta)
    meta_ref[...] = meta

    stack[0:ROWS] = moe_in
    cot = cot_ref[...].astype(single)
    for j in range(2):
        stack[ROWS * (j + 1) : ROWS * (j + 2)] = (gates[j] * cot).astype(bfloat)
    turned = jnp.transpose(meta)
    first, second = turned[0:1, :].astype(jnp.int32), turned[1:2, :].astype(jnp.int32)
    block = 384
    for start in range(0, SLOTS, block):
        slot = iota((block, ROWS), 0) + start
        hot = jnp.concatenate(
            [
                ((slot == first) | (slot == second)).astype(single).astype(bfloat),
                (slot == first + CAP).astype(single).astype(bfloat),
                (slot == second + CAP).astype(single).astype(bfloat),
            ],
            axis=1,
        )
        send_ref[start : start + block] = dot(hot, stack[...]).astype(bfloat)
    for copy in arriving[6:] + leaving:
        copy.wait()


def far(value):
    return pltpu.with_memory_space_constraint(value, pltpu.HBM)


def whole(memory=None):
    return pl.BlockSpec(memory_space=pltpu.VMEM if memory is None else memory)


def forward_part(core, lengths, tokens, cotangent, routes, mine, expert, theirs, packs):
    kept = [((ROWS, WIDTH), bfloat)] * 4 + [
        ((ROWS, WIDTH), single),
        ((ROWS, WIDTH), bfloat),
        ((HEADS, ROWS, ROWS), bfloat),
    ]
    near = [((SLOTS, WIDTH), bfloat), ((ROWS, LANES), single)]
    return pl.pallas_call(
        forward_kernel,
        out_shape=[jax.ShapeDtypeStruct(shape, kind) for shape, kind in near]
        + [pltpu.VMEM((WIDTH, FFH), bfloat), pltpu.VMEM((FFH, WIDTH), bfloat)]
        + [pltpu.HBM(shape, kind) for shape, kind in kept]
        + [pltpu.HBM((HALF, WIDTH), bfloat)] * 4,
        in_specs=[whole(pltpu.SMEM)] * 2 + [whole()] + [whole(pltpu.HBM)] * 8 + [whole()] * 6,
        out_specs=[whole()] * 4 + [whole(pltpu.HBM)] * 11,
        scratch_shapes=[pltpu.VMEM((ROWS, WIDTH), bfloat)] * 2
        + [pltpu.VMEM((HALF, WIDTH), bfloat)] * 4
        + [pltpu.VMEM(shape, kind) for shape, kind in kept]
        + [
            pltpu.VMEM((3 * ROWS, WIDTH), bfloat),
            pltpu.SemaphoreType.DMA((8,)),
            pltpu.SemaphoreType.DMA((11,)),
        ],
        compiler_params=pltpu.CompilerParams(vmem_limit_bytes=FORWARD_LIMIT),
        cost_estimate=pl.CostEstimate(
            flops=5 * 10**9, bytes_accessed=16 * 10**6, transcendentals=10**6
        ),
        name="attention_and_dispatch",
    )(core, lengths, routes, far(tokens), far(cotangent), *map(far, mine + expert), *theirs, *packs)


def gelu_pair(v):
    c = 0.7978845608028654
    square = v * v
    inner = v * (c + (c * 0.044715) * square)
    t = jnp.tanh(inner)
    half = 0.5 * (1.0 + t)
    slope = half + (0.5 * v) * (1.0 - t * t) * (c + (3.0 * c * 0.044715) * square)
    return v * half, slope


def expert_kernel(first, count, rows_ref, up_ref, down_ref, *refs):
    out_ref, act_hbm, gh_hbm, act_ref, gh_ref, sems = refs[-6:]
    total = EXPERTS * CAP
    tokens = slice(first, first + count)
    grads = slice(total + first, total + first + count)
    tile = 256

    def products(start):
        cols = slice(start, start + tile)
        hidden = dot(rows_ref[tokens], up_ref[:, cols])
        return hidden, dot_nt(rows_ref[grads], down_ref[cols])

    ahead, leaving = products(0), []
    for start in range(0, FFH, tile):
        hidden, grad_active = ahead
        if start + tile < FFH:
            ahead = products(start + tile)
        value, slope = gelu_pair(hidden)
        cols = (slice(None), slice(start, start + tile))
        act_ref[cols] = value.astype(bfloat)
        gh_ref[cols] = (grad_active * slope).astype(bfloat)
        leaving += start_all(
            [(act_ref.at[cols], act_hbm.at[cols]), (gh_ref.at[cols], gh_hbm.at[cols])],
            sems,
            2 * (start // tile),
        )
    place = (0,) * (len(out_ref.shape) - 3)
    out_ref[(0,) + place] = dot(act_ref[...], down_ref[...]).astype(bfloat)
    out_ref[(1,) + place] = dot_nt(gh_ref[...], up_ref[...]).astype(bfloat)
    for copy in leaving:
        copy.wait()


def expert_part(rows, up, down, name, part=None, earlier=None):
    total = EXPERTS * CAP
    count = total if part is None else total // 2
    first = 0 if part is None else part * count
    if part is None:
        out_shape, out_spec = (2, total, WIDTH), whole()
    else:
        out_shape = (2, 2, count, WIDTH)
        out_spec = pl.BlockSpec((2, 1, count, WIDTH), lambda i: (0, part, 0, 0))
    operands, in_specs, aliases = [rows, up, down], [whole()] * 3, {}
    if earlier is not None:
        operands.append(earlier)
        in_specs.append(pl.BlockSpec(memory_space=pl.ANY))
        aliases = {3: 0}
    return pl.pallas_call(
        partial(expert_kernel, first, count),
        grid=(1,),
        out_shape=[jax.ShapeDtypeStruct(out_shape, bfloat)]
        + [pltpu.HBM((count, FFH), bfloat)] * 2,
        in_specs=in_specs,
        out_specs=[out_spec, whole(pltpu.HBM), whole(pltpu.HBM)],
        scratch_shapes=[pltpu.VMEM((count, FFH), bfloat)] * 2
        + [pltpu.SemaphoreType.DMA((2 * FFH // 256,))],
        input_output_aliases=aliases,
        compiler_params=pltpu.CompilerParams(vmem_limit_bytes=EXPERT_LIMIT),
        cost_estimate=pl.CostEstimate(
            flops=count * 9 * 10**6, bytes_accessed=14 * 10**6, transcendentals=10**6
        ),
        name=name,
    )(*operands)


def down_grad_kernel(left_a, left_b, left_t, rows_m, rows_t, out_ref):
    total = EXPERTS * CAP
    half = total // 2
    out_ref[...] = (
        dot_tn(left_a[...], rows_m[total : total + half])
        + dot_tn(left_b[...], rows_m[total + half :])
        + dot_tn(left_t[...], rows_t[total:])
    )


def up_grad_kernel(left_a, left_b, left_t, rows_m, rows_t, out_ref, turned):
    total = EXPERTS * CAP
    half = total // 2

    @pl.when(pl.program_id(0) == 0)
    def _():
        turned[:, 0:total] = jnp.transpose(rows_m[0:total])
        turned[:, total:] = jnp.transpose(rows_t[0:total])

    out_ref[...] = (
        dot(turned[:, 0:half], left_a[...])
        + dot(turned[:, half:total], left_b[...])
        + dot(turned[:, total:], left_t[...])
    )


def weight_grad(kernel, left, rows_m, rows_t, turned, name):
    tile = 256
    out_shape = (WIDTH, FFH) if turned else (FFH, WIDTH)
    out_spec = (
        pl.BlockSpec((WIDTH, tile), lambda j: (0, j))
        if turned
        else pl.BlockSpec((tile, WIDTH), lambda j: (j, 0))
    )
    return pl.pallas_call(
        kernel,
        grid=(FFH // tile,),
        out_shape=jax.ShapeDtypeStruct(out_shape, single),
        in_specs=[pl.BlockSpec((value.shape[0], tile), lambda j: (0, j)) for value in left]
        + [pl.BlockSpec((SLOTS, WIDTH), lambda j: (0, 0), pipeline_mode=pl.Buffered(1))] * 2,
        out_specs=out_spec,
        scratch_shapes=[pltpu.VMEM((WIDTH, SLOTS), bfloat)] if turned else [],
        compiler_params=pltpu.CompilerParams(vmem_limit_bytes=GRAD_LIMIT),
        cost_estimate=pl.CostEstimate(
            flops=7 * 10**9, bytes_accessed=14 * 10**6, transcendentals=0
        ),
        name=name,
    )(*left, rows_m, rows_t)


def norm_back(grad, unit, inverse, gain):
    weighted = grad * gain
    center = jnp.mean(weighted * unit, axis=-1, keepdims=True)
    return inverse * (weighted - unit * center), jnp.sum(grad * unit, axis=0, keepdims=True)


def put(total, index, value):
    for lane in range(WIDTH // LANES):
        first = (index * (WIDTH // LANES) + lane) * HALF
        total[first : first + HALF] = value[:, lane * LANES : (lane + 1) * LANES].astype(bfloat)


def backward_kernel(
    core_ref,
    routes_ref,
    meta_ref,
    pack_m,
    pack_t,
    got_hbm,
    cot_hbm,
    res_hbm,
    wo_mh,
    wo_th,
    out_hbm,
    v_hbm,
    probs_hbm,
    k_hbm,
    q_hbm,
    x_hbm,
    low_hbm,
    wq_mh,
    wq_th,
    wk_mh,
    wk_th,
    wv_mh,
    wv_th,
    layer_hbm,
    gtok_hbm,
    sum_m,
    sum_t,
    got_ref,
    cot_ref,
    res_ref,
    wo_m,
    wo_t,
    out_ref,
    v_ref,
    probs_ref,
    k_ref,
    q_ref,
    x_ref,
    low_ref,
    wq_m,
    wq_t,
    wk_m,
    wk_t,
    wv_m,
    wv_t,
    layer_ref,
    gtok_ref,
    wide,
    ga,
    gq,
    gk,
    gv,
    lines,
    small,
    tab,
    in_sems,
    out_sems,
):
    arriving = start_all(
        [
            (got_hbm, got_ref),
            (cot_hbm, cot_ref),
            (res_hbm, res_ref),
            (wo_mh, wo_m),
            (wo_th, wo_t),
            (out_hbm, out_ref),
            (v_hbm, v_ref),
            (probs_hbm, probs_ref),
            (k_hbm, k_ref),
            (q_hbm, q_ref),
            (x_hbm, x_ref),
            (low_hbm, low_ref),
            (wq_mh, wq_m),
            (wq_th, wq_t),
            (wk_mh, wk_m),
            (wk_th, wk_t),
            (wv_mh, wv_m),
            (wv_th, wv_t),
        ],
        in_sems,
    )
    core = core_ref[0]
    mine = pl.ds(pl.multiple_of(core * HALF, HALF), HALF)
    theirs = pl.ds(pl.multiple_of((1 - core) * HALF, HALF), HALF)
    halves = ((mine, sum_m, 0), (theirs, sum_t, 1))
    gain_attn, gain_moe = gain_rows(core, pack_m, pack_t)
    meta = meta_ref[...]
    places = [meta[:, j : j + 1].astype(jnp.int32) for j in range(2)]
    gates = [meta[:, 2 + j : 3 + j] for j in range(2)]
    slot = iota((ROWS, SLOTS), 1)
    hots = [(slot == places[j]).astype(single).astype(bfloat) for j in range(2)]
    hots.append(
        ((slot == places[0] + CAP) | (slot == places[1] + CAP)).astype(single).astype(bfloat)
    )
    for i in range(3):
        arriving[i].wait()
    cot = cot_ref[...].astype(single)
    residual = res_ref[...]
    got = got_ref[...]
    mixed = residual
    grad_gates = []
    for j in range(2):
        picked = dot(hots[j], got)
        mixed = mixed + gates[j] * picked
        grad_gates.append(jnp.sum(cot * picked, axis=1, keepdims=True))
    layer_ref[...] = mixed.astype(bfloat)
    leaving = start_all([(layer_ref, layer_hbm)], out_sems)
    center = gates[0] * grad_gates[0] + gates[1] * grad_gates[1]
    lane = iota((ROWS, LANES), 1)
    grad_logits = jnp.zeros((ROWS, LANES), single)
    for j in range(2):
        grad_logits = grad_logits + jnp.where(
            lane == routes_ref[:, j : j + 1], gates[j] * (grad_gates[j] - center), 0.0
        )
    grad_logits = grad_logits.astype(bfloat)
    wide[...] = dot(hots[2], got)
    for part, pack in ((mine, pack_m), (theirs, pack_t)):
        wide[:, part] += dot_nt(grad_logits, pack[0:HALF, :])
    unit, inverse = unit_rows(residual)
    grad_in, grad_gain_moe = norm_back(wide[...], unit, inverse, gain_moe)
    grad_residual = cot + grad_in
    grad_proj = grad_residual.astype(bfloat)
    for i in range(3, 10):
        arriving[i].wait()
    for (part, total, _), w in zip(halves, (wo_m, wo_t)):
        ga[:, part] = dot_nt(grad_proj, w[...]).astype(bfloat)

    lines[...] = jnp.zeros_like(lines)
    flip = (iota((ROWS, ROWS), 0) + iota((ROWS, ROWS), 1) == ROWS - 1).astype(single)
    flip = flip.astype(bfloat)
    sides, first_side = head_sides()

    def grad_probs_of(h):
        pair = pair_of(h)
        return dot_nt(ga[:, pair] * sides[h % 2], v_ref[:, pair])

    def finish(h, grads):
        pair = pair_of(h)
        keys, asked, mixed = k_ref[:, pair], q_ref[:, pair], ga[:, pair]
        both = [dot(grad, keys) for grad in grads]
        gq[:, pair] = (jnp.where(first_side, *both) * SCALE).astype(bfloat)
        both = [dot_tn(grad, asked) for grad in grads]
        gk[:, pair] = (jnp.where(first_side, *both) * SCALE).astype(bfloat)
        both = [dot_tn(probs_ref[h + i], mixed) for i in range(2)]
        gv[:, pair] = jnp.where(first_side, *both).astype(bfloat)
        for i, grad in enumerate(grads):
            skewed = pltpu.roll(dot(flip, grad), 0, 1, stride=1, stride_axis=0)
            row = TABLE_LANE + 2 + h + i
            lines[row : row + 1, :] = jnp.sum(skewed, axis=0, keepdims=True)

    ahead = grad_probs_of(0)
    done = []
    for h in range(HEADS):
        grad_probs = ahead
        if h + 1 < HEADS:
            ahead = grad_probs_of(h + 1)
        probs = probs_ref[h].astype(single)
        inner = jnp.sum(probs * grad_probs, axis=1, keepdims=True)
        done.append((probs * (grad_probs - inner)).astype(bfloat))
        if h % 2 == 1 and h > 1:
            finish(h - 3, done[h - 3 : h - 1])
    finish(HEADS - 2, done[HEADS - 2 :])

    for i in range(10, 18):
        arriving[i].wait()
    x = x_ref[...].astype(single)
    unit, inverse = unit_rows(x)
    for (part, total, _), wq, wk, wv in zip(
        halves, (wq_m, wq_t), (wk_m, wk_t), (wv_m, wv_t)
    ):
        wide[:, part] = (
            dot_nt(gq[...], wq[...]) + dot_nt(gk[...], wk[...]) + dot_nt(gv[...], wv[...])
        )
    grad_in, grad_gain_attn = norm_back(wide[...], unit, inverse, gain_attn)
    gtok_ref[...] = (grad_residual + grad_in).astype(bfloat)
    leaving += start_all([(gtok_ref, gtok_hbm)], out_sems, 1)

    wide[...] = unit * gain_attn
    for part, total, _ in halves:
        left = wide[:, part].astype(bfloat)
        for i, grad in enumerate((gq, gk, gv)):
            put(total, i, dot_tn(left, grad[...]))
        put(total, 3, dot_tn(out_ref[:, part], grad_proj))

    distance = (ROWS - 1) - iota((NB, ROWS), 1)
    hot = (bucket_of(distance) == iota((NB, ROWS), 0)).astype(single)
    tab[...] = lax.dot_general(
        hot, lines[...], ROWS_ROWS, precision=lax.Precision.HIGHEST, preferred_element_type=single
    )
    row = iota((LANES, WIDTH), 0)
    gains = jnp.where(row == TABLE_LANE, grad_gain_attn, 0.0)
    gains = jnp.where(row == TABLE_LANE + 1, grad_gain_moe, gains)
    small[...] = jnp.transpose(gains)
    for part, total, flag in halves:
        extra = dot_tn(low_ref[:, part], grad_logits) + small[part, :]
        place = core if flag == 0 else 1 - core
        rows = tab[pl.ds(pl.multiple_of(place * 16, 16), 16), :]
        total[EXTRA : EXTRA + 16] = (extra[0:16] + rows).astype(bfloat)
        total[EXTRA + 16 : EXTRA + HALF] = extra[16:].astype(bfloat)
        total[EXTRA + HALF :] = jnp.zeros((DENSE - EXTRA - HALF, LANES), bfloat)
    for copy in leaving:
        copy.wait()


def backward_part(core, tokens, cotangent, routes, meta, got, kept, weights, packs):
    q, k, v, out, res, low, probs = kept
    wq_m, wq_t, wk_m, wk_t, wv_m, wv_t, wo_m, wo_t = weights
    fetched = [got, cotangent, res, wo_m, wo_t, out, v, probs, k, q, tokens, low]
    fetched += [wq_m, wq_t, wk_m, wk_t, wv_m, wv_t]
    return pl.pallas_call(
        backward_kernel,
        out_shape=[pltpu.HBM((ROWS, WIDTH), bfloat)] * 2
        + [jax.ShapeDtypeStruct((DENSE, LANES), bfloat)] * 2,
        in_specs=[whole(pltpu.SMEM)] + [whole()] * 4 + [whole(pltpu.HBM)] * len(fetched),
        out_specs=[whole(pltpu.HBM)] * 2 + [whole()] * 2,
        scratch_shapes=[pltpu.VMEM(value.shape, value.dtype) for value in fetched]
        + [pltpu.VMEM((ROWS, WIDTH), bfloat)] * 2
        + [pltpu.VMEM((ROWS, WIDTH), single)]
        + [pltpu.VMEM((ROWS, WIDTH), bfloat)] * 4
        + [
            pltpu.VMEM((LANES, ROWS), single),
            pltpu.VMEM((WIDTH, LANES), single),
            pltpu.VMEM((NB, LANES), single),
            pltpu.SemaphoreType.DMA((len(fetched),)),
            pltpu.SemaphoreType.DMA((2,)),
        ],
        compiler_params=pltpu.CompilerParams(vmem_limit_bytes=BACKWARD_LIMIT),
        cost_estimate=pl.CostEstimate(
            flops=8 * 10**9, bytes_accessed=20 * 10**6, transcendentals=10**6
        ),
        name="combine_and_backward",
    )(core, routes, meta, *packs, *map(far, fetched))


def unpack_kernel(summed_ref, *refs):
    far_refs, (router_ref, table_ref, first_ref, second_ref) = refs[:4], refs[4:8]
    near_refs, sems = refs[8:12], refs[12]
    leaving = []
    for i in range(4):
        for lane in range(WIDTH // LANES):
            first = (i * (WIDTH // LANES) + lane) * HALF
            near_refs[i][:, lane * LANES : (lane + 1) * LANES] = summed_ref[
                first : first + HALF
            ].astype(single)
        leaving += start_all([(near_refs[i], far_refs[i])], sems, i)
    small = summed_ref[EXTRA : EXTRA + HALF].astype(single)
    turned = jnp.transpose(small)
    router_ref[...] = turned[0:EXPERTS]
    first_ref[...] = turned[TABLE_LANE]
    second_ref[...] = turned[TABLE_LANE + 1]
    table_ref[...] = small[0 : NB // 2, TABLE_LANE + 2 : TABLE_LANE + 2 + HEADS]
    for copy in leaving:
        copy.wait()


def unpack_part(summed):
    shapes = [(EXPERTS, HALF), (NB // 2, HEADS), (HALF,), (HALF,)]
    return pl.pallas_call(
        unpack_kernel,
        out_shape=[pltpu.HBM((HALF, WIDTH), single)] * 4
        + [jax.ShapeDtypeStruct(shape, single) for shape in shapes],
        in_specs=[whole()],
        out_specs=[whole(pltpu.HBM)] * 4 + [whole()] * len(shapes),
        scratch_shapes=[pltpu.VMEM((HALF, WIDTH), single)] * 4 + [pltpu.SemaphoreType.DMA((4,))],
        compiler_params=pltpu.CompilerParams(vmem_limit_bytes=16 * 1024 * 1024),
        cost_estimate=pl.CostEstimate(
            flops=10**6, bytes_accessed=8 * 10**6, transcendentals=0
        ),
        name="unpack_dense_grads",
    )(summed)


def pack_small(w_router, bias_table, attn_gain, moe_gain):
    side = jnp.pad(bias_table, ((0, HALF - NB // 2), (0, LANES - EXPERTS - HEADS)))
    top = jnp.concatenate([w_router, side], axis=1)
    bottom = jnp.concatenate([attn_gain, moe_gain]).reshape(6, LANES)
    return jnp.concatenate([top, jnp.pad(bottom, ((0, 10), (0, 0)))], axis=0)


def per_device(
    tokens,
    lengths,
    routes,
    w_query,
    w_key,
    w_value,
    w_output,
    w_router,
    bias_table,
    attn_gain,
    moe_gain,
    expert_up,
    expert_down,
    cotangent,
):
    core = lax.axis_index("wshard").astype(jnp.int32).reshape(1)

    def swap(value):
        return lax.ppermute(value, "wshard", [(0, 1), (1, 0)])

    pack = pack_small(w_router, bias_table, attn_gain, moe_gain)
    mine = (w_query, w_key, w_value, w_output)
    theirs = [swap(weight) for weight in mine]
    packs = [pack, swap(pack)]
    expert = (expert_up[0], expert_down[0])
    send, meta, up, down, *kept = forward_part(
        core, lengths, tokens, cotangent, routes, mine, expert, theirs, packs
    )
    kept, theirs = kept[:7], kept[7:]
    weights = [half for pair in zip(mine, theirs) for half in pair]

    def exchange(value):
        return lax.all_to_all(value, "expert", split_axis=0, concat_axis=0, tiled=True)

    slots = 2 * CAP
    received = exchange(send.reshape(EXPERTS, slots, WIDTH))
    rows_m = jnp.transpose(received, (1, 0, 2)).reshape(SLOTS, WIDTH)
    rows_t = swap(rows_m)
    half_m, act_a, gh_a = expert_part(rows_m, up, down, "expert_own_rows_a", 0)
    rows_t, half_m = lax.optimization_barrier((rows_t, half_m))
    out_t, act_t, gh_t = expert_part(rows_t, up, down, "expert_other_rows")
    arrived = swap(out_t)
    out_m, act_b, gh_b = expert_part(rows_m, up, down, "expert_own_rows_b", 1, half_m)
    result = out_m.reshape(SLOTS, WIDTH).astype(single)
    result = (result + arrived.reshape(SLOTS, WIDTH).astype(single)).astype(bfloat)
    result = lax.optimization_barrier(result)
    result = jnp.transpose(result.reshape(slots, EXPERTS, WIDTH), (1, 0, 2))
    result, act_t, gh_t = lax.optimization_barrier((result, act_t, gh_t))
    got = exchange(result).reshape(SLOTS, WIDTH)
    grad_down = weight_grad(
        down_grad_kernel, (act_a, act_b, act_t), rows_m, rows_t, False, "expert_down_grad"
    )
    grad_up = weight_grad(
        up_grad_kernel, (gh_a, gh_b, gh_t), rows_m, rows_t, True, "expert_up_grad"
    )
    got, grad_down, grad_up = lax.optimization_barrier((got, grad_down, grad_up))
    layer_out, grad_tokens, sum_m, sum_t = backward_part(
        core, tokens, cotangent, routes, meta, got, kept, weights, packs
    )
    pair = (sum_m.astype(single) + swap(sum_t).astype(single)).astype(bfloat)
    pieces = exchange(pair.reshape(EXPERTS, DENSE // EXPERTS, LANES))
    piece = jnp.sum(pieces.astype(single), axis=0).astype(bfloat)
    summed = exchange(jnp.broadcast_to(piece[None], pieces.shape))
    *dense, router, table, first_gain, second_gain = unpack_part(summed.reshape(DENSE, LANES))
    return (
        layer_out,
        grad_tokens,
        *dense,
        router.T,
        table,
        first_gain,
        second_gain,
        grad_up[None],
        grad_down[None],
    )


def solution(mesh):
    in_specs = (
        P(("expert", "wshard"), None),
        P(("expert", "wshard"), None),
        P(("expert", "wshard"), None),
        P("wshard", None),
        P("wshard", None),
        P("wshard", None),
        P("wshard", None),
        P("wshard", None),
        P("wshard", None),
        P("wshard"),
        P("wshard"),
        P("expert", None, "wshard"),
        P("expert", "wshard", None),
        P(("expert", "wshard"), None),
    )
    out_specs = (
        P(("expert", "wshard"), None),
        P(("expert", "wshard"), None),
        P("wshard", None),
        P("wshard", None),
        P("wshard", None),
        P("wshard", None),
        P("wshard", None),
        P("wshard", None),
        P("wshard"),
        P("wshard"),
        P("expert", None, "wshard"),
        P("expert", "wshard", None),
    )
    return jax.shard_map(
        per_device, mesh=mesh, in_specs=in_specs, out_specs=out_specs, check_vma=False
    )
```

```python
from functools import partial

import jax
import jax.numpy as jnp
import numpy as np
from jax import lax
from jax.experimental import pallas as pl
from jax.experimental.pallas import tpu as pltpu
from jax.sharding import PartitionSpec as P

ROWS = 256
WIDTH = 768
HALF = 384
HEADS = 12
HEAD = 64
NB = 32
CAP = 12
EXPERTS = 64
SLOTS = EXPERTS * 2 * CAP
FFH = 1536
LANES = 128
TABLE_LANE = 64
GAIN_ROW = 384
EXTRA = 4 * HALF * WIDTH // LANES
DENSE = EXPERTS * 152
SCALE = HEAD ** (-0.5)
NEG = -1000000000.0
EPS = 1e-06
FORWARD_LIMIT = 32 * 1024 * 1024
EXPERT_LIMIT = 26 * 1024 * 1024
GRAD_LIMIT = 16 * 1024 * 1024
BACKWARD_LIMIT = 36 * 1024 * 1024

bfloat = jnp.bfloat16
single = jnp.float32
THRESHOLDS = [int(16 * 8.0 ** (j / 16)) for j in range(1, 16)]

ROWS_ROWS = (((1,), (1,)), ((), ()))
COLS_COLS = (((0,), (0,)), ((), ()))


def dot(a, b):
    return jnp.dot(a, b, preferred_element_type=single)


def dot_nt(a, b):
    return lax.dot_general(a, b, ROWS_ROWS, preferred_element_type=single)


def dot_tn(a, b):
    return lax.dot_general(a, b, COLS_COLS, preferred_element_type=single)


def iota(shape, dim):
    return lax.broadcasted_iota(jnp.int32, shape, dim)


def bucket_of(distance):
    beyond = jnp.zeros_like(distance)
    for threshold in THRESHOLDS:
        beyond = beyond + (distance >= threshold).astype(jnp.int32)
    return jnp.where(distance < 16, distance, 16 + beyond)


def in_order(core, mine, theirs, axis):
    return jnp.where(
        core == 0,
        jnp.concatenate([mine, theirs], axis=axis),
        jnp.concatenate([theirs, mine], axis=axis),
    )


def gain_rows(core, pack_mine, pack_theirs):
    gains = []
    mine = pack_mine[GAIN_ROW : GAIN_ROW + 16, :].astype(single)
    theirs = pack_theirs[GAIN_ROW : GAIN_ROW + 16, :].astype(single)
    for first in (0, 3):
        rows = [
            jnp.concatenate([block[first + i : first + i + 1] for i in range(3)], axis=1)
            for block in (mine, theirs)
        ]
        gains.append(in_order(core, rows[0], rows[1], 1))
    return gains


def unit_rows(value):
    inverse = lax.rsqrt(jnp.mean(value * value, axis=-1, keepdims=True) + EPS)
    return value * inverse, inverse


def pair_of(h):
    return slice((h // 2) * 2 * HEAD, (h // 2 + 1) * 2 * HEAD)


def head_sides():
    lane = iota((1, 2 * HEAD), 1)
    first = (lane < HEAD).astype(single)
    return (first.astype(bfloat), (1.0 - first).astype(bfloat)), lane < HEAD


def start_all(pairs, sems, first=0):
    copies = [
        pltpu.make_async_copy(src, dst, sems.at[first + i]) for i, (src, dst) in enumerate(pairs)
    ]
    for copy in copies:
        copy.start()
    return copies


def forward_kernel(
    core_ref,
    len_ref,
    routes_ref,
    x_hbm,
    cot_hbm,
    wq_mh,
    wk_mh,
    wv_mh,
    wo_mh,
    up_hbm,
    down_hbm,
    wq_t,
    wk_t,
    wv_t,
    wo_t,
    pack_m,
    pack_t,
    send_ref,
    meta_ref,
    up_near,
    down_near,
    q_hbm,
    k_hbm,
    v_hbm,
    out_hbm,
    res_hbm,
    low_hbm,
    probs_hbm,
    wq_th,
    wk_th,
    wv_th,
    wo_th,
    x_ref,
    cot_ref,
    wq_m,
    wk_m,
    wv_m,
    wo_m,
    q_ref,
    k_ref,
    v_ref,
    out_ref,
    res_ref,
    low_ref,
    probs_ref,
    stack,
    in_sems,
    out_sems,
):
    arriving = start_all(
        [
            (x_hbm, x_ref),
            (wq_mh, wq_m),
            (wk_mh, wk_m),
            (wv_mh, wv_m),
            (wo_mh, wo_m),
            (cot_hbm, cot_ref),
        ],
        in_sems,
    )
    core = core_ref[0]
    mine = pl.ds(pl.multiple_of(core * HALF, HALF), HALF)
    theirs = pl.ds(pl.multiple_of((1 - core) * HALF, HALF), HALF)
    gain_attn, gain_moe = gain_rows(core, pack_m, pack_t)
    row, col = iota((ROWS, ROWS), 0), iota((ROWS, ROWS), 1)
    seg_row, seg_col = jnp.zeros_like(row), jnp.zeros_like(col)
    edge = 0
    for i in range(4):
        edge = edge + len_ref[0, i]
        seg_row = seg_row + (row >= edge).astype(jnp.int32)
        seg_col = seg_col + (col >= edge).astype(jnp.int32)
    allowed = (seg_row == seg_col) & (col <= row)
    distance = (ROWS - iota((NB, ROWS), 1)) % ROWS
    hot = (bucket_of(distance) == iota((NB, ROWS), 0)).astype(single).astype(bfloat)
    table = in_order(core, pack_m[0:16, :].astype(single), pack_t[0:16, :].astype(single), 0)
    by_distance = dot_tn(table.astype(bfloat), hot)

    lane = iota((ROWS, LANES), 1)
    chosen = [(lane == routes_ref[:, j : j + 1]).astype(single) for j in range(2)]
    earlier = (col < row).astype(single).astype(bfloat)
    before = dot(earlier, (chosen[0] + chosen[1]).astype(bfloat))
    places = []
    for j in range(2):
        slot = jnp.sum(before * chosen[j], axis=1, keepdims=True)
        places.append(routes_ref[:, j : j + 1].astype(single) * (2 * CAP) + slot)
    arriving[0].wait()
    x = x_ref[...].astype(single)
    low_ref[...] = (unit_rows(x)[0] * gain_attn).astype(bfloat)
    own, other = low_ref[:, mine], low_ref[:, theirs]
    for i, (ref, w_m, w_t) in enumerate(
        ((q_ref, wq_m, wq_t), (k_ref, wk_m, wk_t), (v_ref, wv_m, wv_t))
    ):
        arriving[1 + i].wait()
        ref[...] = (dot(own, w_m[...]) + dot(other, w_t[...])).astype(bfloat)
    arriving += start_all([(up_hbm, up_near), (down_hbm, down_near)], in_sems, 6)
    leaving = start_all([(q_ref, q_hbm), (k_ref, k_hbm), (v_ref, v_hbm)], out_sems)
    leaving += start_all(
        [(wq_t, wq_th), (wk_t, wk_th), (wv_t, wv_th), (wo_t, wo_th)], out_sems, 7
    )

    sides, first_side = head_sides()

    def raw_scores(h):
        pair = pair_of(h)
        return dot_nt(q_ref[:, pair] * sides[h % 2], k_ref[:, pair])

    def finish(h):
        pair = pair_of(h)
        values = v_ref[:, pair]
        mixed = jnp.where(first_side, dot(probs_ref[h], values), dot(probs_ref[h + 1], values))
        out_ref[:, pair] = mixed.astype(bfloat)

    ahead = raw_scores(0)
    for h in range(HEADS):
        raw = ahead
        if h + 1 < HEADS:
            ahead = raw_scores(h + 1)
        line = by_distance[TABLE_LANE + h : TABLE_LANE + h + 1, :]
        bias = pltpu.roll(
            jnp.broadcast_to(line, (ROWS, ROWS)), 0, 1, stride=1, stride_axis=0
        )
        scores = jnp.where(allowed, raw * SCALE + bias, NEG)
        exponent = jnp.exp(scores - jnp.max(scores, axis=1, keepdims=True))
        low = (exponent * (1.0 / jnp.sum(exponent, axis=1, keepdims=True))).astype(bfloat)
        probs_ref[h] = low
        if h % 2 == 1 and h > 1:
            finish(h - 3)
    finish(HEADS - 2)

    leaving += start_all([(probs_ref, probs_hbm), (out_ref, out_hbm)], out_sems, 3)
    for copy in arriving[4:6]:
        copy.wait()
    residual = x + dot(out_ref[:, mine], wo_m[...]) + dot(out_ref[:, theirs], wo_t[...])
    res_ref[...] = residual
    moe_in = (unit_rows(residual)[0] * gain_moe).astype(bfloat)
    low_ref[...] = moe_in
    leaving += start_all([(res_ref, res_hbm), (low_ref, low_hbm)], out_sems, 5)
    logits = dot(low_ref[:, mine], pack_m[0:HALF, :]) + dot(
        low_ref[:, theirs], pack_t[0:HALF, :]
    )
    pair_logits = []
    for j in range(2):
        pair_logits.append(
            jnp.sum(jnp.where(chosen[j] > 0, logits, 0.0), axis=1, keepdims=True)
        )
    peak = jnp.maximum(pair_logits[0], pair_logits[1])
    powers = [jnp.exp(value - peak) for value in pair_logits]
    gates = [power / (powers[0] + powers[1]) for power in powers]
    meta = jnp.zeros((ROWS, LANES), single)
    for i, column in enumerate(places + gates):
        meta = jnp.where(lane == i, column, meta)
    meta_ref[...] = meta

    stack[0:ROWS] = moe_in
    cot = cot_ref[...].astype(single)
    for j in range(2):
        stack[ROWS * (j + 1) : ROWS * (j + 2)] = (gates[j] * cot).astype(bfloat)
    turned = jnp.transpose(meta)
    first, second = turned[0:1, :].astype(jnp.int32), turned[1:2, :].astype(jnp.int32)
    block = 384
    for start in range(0, SLOTS, block):
        slot = iota((block, ROWS), 0) + start
        hot = jnp.concatenate(
            [
                ((slot == first) | (slot == second)).astype(single).astype(bfloat),
                (slot == first + CAP).astype(single).astype(bfloat),
                (slot == second + CAP).astype(single).astype(bfloat),
            ],
            axis=1,
        )
        send_ref[start : start + block] = dot(hot, stack[...]).astype(bfloat)
    for copy in arriving[6:] + leaving:
        copy.wait()


def far(value):
    return pltpu.with_memory_space_constraint(value, pltpu.HBM)


def whole(memory=None):
    return pl.BlockSpec(memory_space=pltpu.VMEM if memory is None else memory)


def forward_part(core, lengths, tokens, cotangent, routes, mine, expert, theirs, packs):
    kept = [((ROWS, WIDTH), bfloat)] * 4 + [
        ((ROWS, WIDTH), single),
        ((ROWS, WIDTH), bfloat),
        ((HEADS, ROWS, ROWS), bfloat),
    ]
    near = [((SLOTS, WIDTH), bfloat), ((ROWS, LANES), single)]
    return pl.pallas_call(
        forward_kernel,
        out_shape=[jax.ShapeDtypeStruct(shape, kind) for shape, kind in near]
        + [pltpu.VMEM((WIDTH, FFH), bfloat), pltpu.VMEM((FFH, WIDTH), bfloat)]
        + [pltpu.HBM(shape, kind) for shape, kind in kept]
        + [pltpu.HBM((HALF, WIDTH), bfloat)] * 4,
        in_specs=[whole(pltpu.SMEM)] * 2 + [whole()] + [whole(pltpu.HBM)] * 8 + [whole()] * 6,
        out_specs=[whole()] * 4 + [whole(pltpu.HBM)] * 11,
        scratch_shapes=[pltpu.VMEM((ROWS, WIDTH), bfloat)] * 2
        + [pltpu.VMEM((HALF, WIDTH), bfloat)] * 4
        + [pltpu.VMEM(shape, kind) for shape, kind in kept]
        + [
            pltpu.VMEM((3 * ROWS, WIDTH), bfloat),
            pltpu.SemaphoreType.DMA((8,)),
            pltpu.SemaphoreType.DMA((11,)),
        ],
        compiler_params=pltpu.CompilerParams(vmem_limit_bytes=FORWARD_LIMIT),
        cost_estimate=pl.CostEstimate(
            flops=5 * 10**9, bytes_accessed=16 * 10**6, transcendentals=10**6
        ),
        name="attention_and_dispatch",
    )(core, far(lengths), routes, far(tokens), far(cotangent), *map(far, mine + expert), *theirs, *packs)


def gelu_pair(v):
    c = 0.7978845608028654
    square = v * v
    inner = v * (c + (c * 0.044715) * square)
    t = jnp.tanh(inner)
    half = 0.5 * (1.0 + t)
    slope = half + (0.5 * v) * (1.0 - t * t) * (c + (3.0 * c * 0.044715) * square)
    return v * half, slope


def expert_kernel(first, count, rows_ref, up_ref, down_ref, *refs):
    out_ref, act_hbm, gh_hbm, act_ref, gh_ref, sems = refs[-6:]
    total = EXPERTS * CAP
    tokens = slice(first, first + count)
    grads = slice(total + first, total + first + count)
    tile = 256

    def products(start):
        cols = slice(start, start + tile)
        hidden = dot(rows_ref[tokens], up_ref[:, cols])
        return hidden, dot_nt(rows_ref[grads], down_ref[cols])

    ahead, leaving = products(0), []
    for start in range(0, FFH, tile):
        hidden, grad_active = ahead
        if start + tile < FFH:
            ahead = products(start + tile)
        value, slope = gelu_pair(hidden)
        cols = (slice(None), slice(start, start + tile))
        act_ref[cols] = value.astype(bfloat)
        gh_ref[cols] = (grad_active * slope).astype(bfloat)
        leaving += start_all(
            [(act_ref.at[cols], act_hbm.at[cols]), (gh_ref.at[cols], gh_hbm.at[cols])],
            sems,
            2 * (start // tile),
        )
    place = (0,) * (len(out_ref.shape) - 3)
    out_ref[(0,) + place] = dot(act_ref[...], down_ref[...]).astype(bfloat)
    out_ref[(1,) + place] = dot_nt(gh_ref[...], up_ref[...]).astype(bfloat)
    for copy in leaving:
        copy.wait()


def expert_part(rows, up, down, name, part=None, earlier=None):
    total = EXPERTS * CAP
    count = total if part is None else total // 2
    first = 0 if part is None else part * count
    if part is None:
        out_shape, out_spec = (2, total, WIDTH), whole()
    else:
        out_shape = (2, 2, count, WIDTH)
        out_spec = pl.BlockSpec((2, 1, count, WIDTH), lambda i: (0, part, 0, 0))
    operands, in_specs, aliases = [rows, up, down], [whole()] * 3, {}
    if earlier is not None:
        operands.append(earlier)
        in_specs.append(pl.BlockSpec(memory_space=pl.ANY))
        aliases = {3: 0}
    return pl.pallas_call(
        partial(expert_kernel, first, count),
        grid=(1,),
        out_shape=[jax.ShapeDtypeStruct(out_shape, bfloat)]
        + [pltpu.HBM((count, FFH), bfloat)] * 2,
        in_specs=in_specs,
        out_specs=[out_spec, whole(pltpu.HBM), whole(pltpu.HBM)],
        scratch_shapes=[pltpu.VMEM((count, FFH), bfloat)] * 2
        + [pltpu.SemaphoreType.DMA((2 * FFH // 256,))],
        input_output_aliases=aliases,
        compiler_params=pltpu.CompilerParams(vmem_limit_bytes=EXPERT_LIMIT),
        cost_estimate=pl.CostEstimate(
            flops=count * 9 * 10**6, bytes_accessed=14 * 10**6, transcendentals=10**6
        ),
        name=name,
    )(*operands)


def down_grad_kernel(left_a, left_b, left_t, rows_m, rows_t, out_ref):
    total = EXPERTS * CAP
    half = total // 2
    out_ref[...] = (
        dot_tn(left_a[...], rows_m[total : total + half])
        + dot_tn(left_b[...], rows_m[total + half :])
        + dot_tn(left_t[...], rows_t[total:])
    )


def up_grad_kernel(left_a, left_b, left_t, rows_m, rows_t, out_ref, turned):
    total = EXPERTS * CAP
    half = total // 2

    @pl.when(pl.program_id(0) == 0)
    def _():
        turned[:, 0:total] = jnp.transpose(rows_m[0:total])
        turned[:, total:] = jnp.transpose(rows_t[0:total])

    out_ref[...] = (
        dot(turned[:, 0:half], left_a[...])
        + dot(turned[:, half:total], left_b[...])
        + dot(turned[:, total:], left_t[...])
    )


def weight_grad(kernel, left, rows_m, rows_t, turned, name):
    tile = 256
    out_shape = (WIDTH, FFH) if turned else (FFH, WIDTH)
    out_spec = (
        pl.BlockSpec((WIDTH, tile), lambda j: (0, j))
        if turned
        else pl.BlockSpec((tile, WIDTH), lambda j: (j, 0))
    )
    return pl.pallas_call(
        kernel,
        grid=(FFH // tile,),
        out_shape=jax.ShapeDtypeStruct(out_shape, single),
        in_specs=[pl.BlockSpec((value.shape[0], tile), lambda j: (0, j)) for value in left]
        + [pl.BlockSpec((SLOTS, WIDTH), lambda j: (0, 0), pipeline_mode=pl.Buffered(1))] * 2,
        out_specs=out_spec,
        scratch_shapes=[pltpu.VMEM((WIDTH, SLOTS), bfloat)] if turned else [],
        compiler_params=pltpu.CompilerParams(vmem_limit_bytes=GRAD_LIMIT),
        cost_estimate=pl.CostEstimate(
            flops=7 * 10**9, bytes_accessed=14 * 10**6, transcendentals=0
        ),
        name=name,
    )(*left, rows_m, rows_t)


def norm_back(grad, unit, inverse, gain):
    weighted = grad * gain
    center = jnp.mean(weighted * unit, axis=-1, keepdims=True)
    return inverse * (weighted - unit * center), jnp.sum(grad * unit, axis=0, keepdims=True)


def put(total, index, value):
    for lane in range(WIDTH // LANES):
        first = (index * (WIDTH // LANES) + lane) * HALF
        total[first : first + HALF] = value[:, lane * LANES : (lane + 1) * LANES].astype(bfloat)


def backward_kernel(
    core_ref,
    routes_ref,
    meta_ref,
    pack_m,
    pack_t,
    got_hbm,
    cot_hbm,
    res_hbm,
    wo_mh,
    wo_th,
    out_hbm,
    v_hbm,
    probs_hbm,
    k_hbm,
    q_hbm,
    x_hbm,
    low_hbm,
    wq_mh,
    wq_th,
    wk_mh,
    wk_th,
    wv_mh,
    wv_th,
    layer_hbm,
    gtok_hbm,
    sum_m,
    sum_t,
    got_ref,
    cot_ref,
    res_ref,
    wo_m,
    wo_t,
    out_ref,
    v_ref,
    probs_ref,
    k_ref,
    q_ref,
    x_ref,
    low_ref,
    wq_m,
    wq_t,
    wk_m,
    wk_t,
    wv_m,
    wv_t,
    layer_ref,
    gtok_ref,
    wide,
    ga,
    gq,
    gk,
    gv,
    lines,
    small,
    tab,
    in_sems,
    out_sems,
):
    arriving = start_all(
        [
            (got_hbm, got_ref),
            (cot_hbm, cot_ref),
            (res_hbm, res_ref),
            (wo_mh, wo_m),
            (wo_th, wo_t),
            (out_hbm, out_ref),
            (v_hbm, v_ref),
            (probs_hbm, probs_ref),
            (k_hbm, k_ref),
            (q_hbm, q_ref),
            (x_hbm, x_ref),
            (low_hbm, low_ref),
            (wq_mh, wq_m),
            (wq_th, wq_t),
            (wk_mh, wk_m),
            (wk_th, wk_t),
            (wv_mh, wv_m),
            (wv_th, wv_t),
        ],
        in_sems,
    )
    core = core_ref[0]
    mine = pl.ds(pl.multiple_of(core * HALF, HALF), HALF)
    theirs = pl.ds(pl.multiple_of((1 - core) * HALF, HALF), HALF)
    halves = ((mine, sum_m, 0), (theirs, sum_t, 1))
    gain_attn, gain_moe = gain_rows(core, pack_m, pack_t)
    meta = meta_ref[...]
    places = [meta[:, j : j + 1].astype(jnp.int32) for j in range(2)]
    gates = [meta[:, 2 + j : 3 + j] for j in range(2)]
    slot = iota((ROWS, SLOTS), 1)
    hots = [(slot == places[j]).astype(single).astype(bfloat) for j in range(2)]
    hots.append(
        ((slot == places[0] + CAP) | (slot == places[1] + CAP)).astype(single).astype(bfloat)
    )
    for i in range(3):
        arriving[i].wait()
    cot = cot_ref[...].astype(single)
    residual = res_ref[...]
    got = got_ref[...]
    mixed = residual
    grad_gates = []
    for j in range(2):
        picked = dot(hots[j], got)
        mixed = mixed + gates[j] * picked
        grad_gates.append(jnp.sum(cot * picked, axis=1, keepdims=True))
    layer_ref[...] = mixed.astype(bfloat)
    leaving = start_all([(layer_ref, layer_hbm)], out_sems)
    center = gates[0] * grad_gates[0] + gates[1] * grad_gates[1]
    lane = iota((ROWS, LANES), 1)
    grad_logits = jnp.zeros((ROWS, LANES), single)
    for j in range(2):
        grad_logits = grad_logits + jnp.where(
            lane == routes_ref[:, j : j + 1], gates[j] * (grad_gates[j] - center), 0.0
        )
    grad_logits = grad_logits.astype(bfloat)
    wide[...] = dot(hots[2], got)
    for part, pack in ((mine, pack_m), (theirs, pack_t)):
        wide[:, part] += dot_nt(grad_logits, pack[0:HALF, :])
    unit, inverse = unit_rows(residual)
    grad_in, grad_gain_moe = norm_back(wide[...], unit, inverse, gain_moe)
    grad_residual = cot + grad_in
    grad_proj = grad_residual.astype(bfloat)
    for i in range(3, 10):
        arriving[i].wait()
    for (part, total, _), w in zip(halves, (wo_m, wo_t)):
        ga[:, part] = dot_nt(grad_proj, w[...]).astype(bfloat)

    lines[...] = jnp.zeros_like(lines)
    flip = (iota((ROWS, ROWS), 0) + iota((ROWS, ROWS), 1) == ROWS - 1).astype(single)
    flip = flip.astype(bfloat)
    sides, first_side = head_sides()

    def grad_probs_of(h):
        pair = pair_of(h)
        return dot_nt(ga[:, pair] * sides[h % 2], v_ref[:, pair])

    def finish(h, grads):
        pair = pair_of(h)
        keys, asked, mixed = k_ref[:, pair], q_ref[:, pair], ga[:, pair]
        both = [dot(grad, keys) for grad in grads]
        gq[:, pair] = (jnp.where(first_side, *both) * SCALE).astype(bfloat)
        both = [dot_tn(grad, asked) for grad in grads]
        gk[:, pair] = (jnp.where(first_side, *both) * SCALE).astype(bfloat)
        both = [dot_tn(probs_ref[h + i], mixed) for i in range(2)]
        gv[:, pair] = jnp.where(first_side, *both).astype(bfloat)
        for i, grad in enumerate(grads):
            skewed = pltpu.roll(dot(flip, grad), 0, 1, stride=1, stride_axis=0)
            row = TABLE_LANE + 2 + h + i
            lines[row : row + 1, :] = jnp.sum(skewed, axis=0, keepdims=True)

    ahead = grad_probs_of(0)
    done = []
    for h in range(HEADS):
        grad_probs = ahead
        if h + 1 < HEADS:
            ahead = grad_probs_of(h + 1)
        probs = probs_ref[h].astype(single)
        inner = jnp.sum(probs * grad_probs, axis=1, keepdims=True)
        done.append((probs * (grad_probs - inner)).astype(bfloat))
        if h % 2 == 1 and h > 1:
            finish(h - 3, done[h - 3 : h - 1])
    finish(HEADS - 2, done[HEADS - 2 :])

    for i in range(10, 18):
        arriving[i].wait()
    x = x_ref[...].astype(single)
    unit, inverse = unit_rows(x)
    for (part, total, _), wq, wk, wv in zip(
        halves, (wq_m, wq_t), (wk_m, wk_t), (wv_m, wv_t)
    ):
        wide[:, part] = (
            dot_nt(gq[...], wq[...]) + dot_nt(gk[...], wk[...]) + dot_nt(gv[...], wv[...])
        )
    grad_in, grad_gain_attn = norm_back(wide[...], unit, inverse, gain_attn)
    gtok_ref[...] = (grad_residual + grad_in).astype(bfloat)
    leaving += start_all([(gtok_ref, gtok_hbm)], out_sems, 1)

    wide[...] = unit * gain_attn
    for part, total, _ in halves:
        left = wide[:, part].astype(bfloat)
        for i, grad in enumerate((gq, gk, gv)):
            put(total, i, dot_tn(left, grad[...]))
        put(total, 3, dot_tn(out_ref[:, part], grad_proj))

    distance = (ROWS - 1) - iota((NB, ROWS), 1)
    hot = (bucket_of(distance) == iota((NB, ROWS), 0)).astype(single)
    tab[...] = lax.dot_general(
        hot, lines[...], ROWS_ROWS, precision=lax.Precision.HIGHEST, preferred_element_type=single
    )
    row = iota((LANES, WIDTH), 0)
    gains = jnp.where(row == TABLE_LANE, grad_gain_attn, 0.0)
    gains = jnp.where(row == TABLE_LANE + 1, grad_gain_moe, gains)
    small[...] = jnp.transpose(gains)
    for part, total, flag in halves:
        extra = dot_tn(low_ref[:, part], grad_logits) + small[part, :]
        place = core if flag == 0 else 1 - core
        rows = tab[pl.ds(pl.multiple_of(place * 16, 16), 16), :]
        total[EXTRA : EXTRA + 16] = (extra[0:16] + rows).astype(bfloat)
        total[EXTRA + 16 : EXTRA + HALF] = extra[16:].astype(bfloat)
        total[EXTRA + HALF :] = jnp.zeros((DENSE - EXTRA - HALF, LANES), bfloat)
    for copy in leaving:
        copy.wait()


def backward_part(core, tokens, cotangent, routes, meta, got, kept, weights, packs):
    q, k, v, out, res, low, probs = kept
    wq_m, wq_t, wk_m, wk_t, wv_m, wv_t, wo_m, wo_t = weights
    fetched = [got, cotangent, res, wo_m, wo_t, out, v, probs, k, q, tokens, low]
    fetched += [wq_m, wq_t, wk_m, wk_t, wv_m, wv_t]
    return pl.pallas_call(
        backward_kernel,
        out_shape=[pltpu.HBM((ROWS, WIDTH), bfloat)] * 2
        + [jax.ShapeDtypeStruct((DENSE, LANES), bfloat)] * 2,
        in_specs=[whole(pltpu.SMEM)] + [whole()] * 4 + [whole(pltpu.HBM)] * len(fetched),
        out_specs=[whole(pltpu.HBM)] * 2 + [whole()] * 2,
        scratch_shapes=[pltpu.VMEM(value.shape, value.dtype) for value in fetched]
        + [pltpu.VMEM((ROWS, WIDTH), bfloat)] * 2
        + [pltpu.VMEM((ROWS, WIDTH), single)]
        + [pltpu.VMEM((ROWS, WIDTH), bfloat)] * 4
        + [
            pltpu.VMEM((LANES, ROWS), single),
            pltpu.VMEM((WIDTH, LANES), single),
            pltpu.VMEM((NB, LANES), single),
            pltpu.SemaphoreType.DMA((len(fetched),)),
            pltpu.SemaphoreType.DMA((2,)),
        ],
        compiler_params=pltpu.CompilerParams(vmem_limit_bytes=BACKWARD_LIMIT),
        cost_estimate=pl.CostEstimate(
            flops=8 * 10**9, bytes_accessed=20 * 10**6, transcendentals=10**6
        ),
        name="combine_and_backward",
    )(core, routes, meta, *packs, *map(far, fetched))


def unpack_kernel(summed_ref, *refs):
    router_ref, table_ref, first_ref, second_ref = refs[4:]
    for i in range(4):
        for lane in range(WIDTH // LANES):
            first = (i * (WIDTH // LANES) + lane) * HALF
            refs[i][:, lane * LANES : (lane + 1) * LANES] = summed_ref[
                first : first + HALF
            ].astype(single)
    small = summed_ref[EXTRA : EXTRA + HALF].astype(single)
    turned = jnp.transpose(small)
    router_ref[...] = turned[0:EXPERTS]
    first_ref[...] = turned[TABLE_LANE]
    second_ref[...] = turned[TABLE_LANE + 1]
    table_ref[...] = small[0 : NB // 2, TABLE_LANE + 2 : TABLE_LANE + 2 + HEADS]


def unpack_part(summed):
    shapes = [(HALF, WIDTH)] * 4 + [(EXPERTS, HALF), (NB // 2, HEADS), (HALF,), (HALF,)]
    return pl.pallas_call(
        unpack_kernel,
        out_shape=[jax.ShapeDtypeStruct(shape, single) for shape in shapes],
        in_specs=[whole()],
        out_specs=[whole()] * len(shapes),
        compiler_params=pltpu.CompilerParams(vmem_limit_bytes=16 * 1024 * 1024),
        cost_estimate=pl.CostEstimate(
            flops=10**6, bytes_accessed=8 * 10**6, transcendentals=0
        ),
        name="unpack_dense_grads",
    )(summed)


def pack_small(w_router, bias_table, attn_gain, moe_gain):
    side = jnp.pad(bias_table, ((0, HALF - NB // 2), (0, LANES - EXPERTS - HEADS)))
    top = jnp.concatenate([w_router, side], axis=1)
    bottom = jnp.concatenate([attn_gain, moe_gain]).reshape(6, LANES)
    return jnp.concatenate([top, jnp.pad(bottom, ((0, 10), (0, 0)))], axis=0)


def per_device(
    tokens,
    lengths,
    routes,
    w_query,
    w_key,
    w_value,
    w_output,
    w_router,
    bias_table,
    attn_gain,
    moe_gain,
    expert_up,
    expert_down,
    cotangent,
):
    core = lax.axis_index("wshard").astype(jnp.int32).reshape(1)

    def swap(value):
        return lax.ppermute(value, "wshard", [(0, 1), (1, 0)])

    pack = pack_small(w_router, bias_table, attn_gain, moe_gain)
    mine = (w_query, w_key, w_value, w_output)
    theirs = [swap(weight) for weight in mine]
    packs = [pack, swap(pack)]
    expert = (expert_up[0], expert_down[0])
    send, meta, up, down, *kept = forward_part(
        core, lengths, tokens, cotangent, routes, mine, expert, theirs, packs
    )
    kept, theirs = kept[:7], kept[7:]
    weights = [half for pair in zip(mine, theirs) for half in pair]

    def exchange(value):
        return lax.all_to_all(value, "expert", split_axis=0, concat_axis=0, tiled=True)

    slots = 2 * CAP
    received = exchange(send.reshape(EXPERTS, slots, WIDTH))
    rows_m = jnp.transpose(received, (1, 0, 2)).reshape(SLOTS, WIDTH)
    rows_t = swap(rows_m)
    half_m, act_a, gh_a = expert_part(rows_m, up, down, "expert_own_rows_a", 0)
    rows_t, half_m = lax.optimization_barrier((rows_t, half_m))
    out_t, act_t, gh_t = expert_part(rows_t, up, down, "expert_other_rows")
    arrived = swap(out_t)
    out_m, act_b, gh_b = expert_part(rows_m, up, down, "expert_own_rows_b", 1, half_m)
    result = out_m.reshape(SLOTS, WIDTH).astype(single)
    result = (result + arrived.reshape(SLOTS, WIDTH).astype(single)).astype(bfloat)
    result = lax.optimization_barrier(result)
    result = jnp.transpose(result.reshape(slots, EXPERTS, WIDTH), (1, 0, 2))
    result, act_t, gh_t = lax.optimization_barrier((result, act_t, gh_t))
    got = exchange(result).reshape(SLOTS, WIDTH)
    grad_down = weight_grad(
        down_grad_kernel, (act_a, act_b, act_t), rows_m, rows_t, False, "expert_down_grad"
    )
    grad_up = weight_grad(
        up_grad_kernel, (gh_a, gh_b, gh_t), rows_m, rows_t, True, "expert_up_grad"
    )
    got, grad_down, grad_up = lax.optimization_barrier((got, grad_down, grad_up))
    layer_out, grad_tokens, sum_m, sum_t = backward_part(
        core, tokens, cotangent, routes, meta, got, kept, weights, packs
    )
    pair = (sum_m.astype(single) + swap(sum_t).astype(single)).astype(bfloat)
    pieces = exchange(pair.reshape(EXPERTS, DENSE // EXPERTS, LANES))
    piece = jnp.sum(pieces.astype(single), axis=0).astype(bfloat)
    summed = exchange(jnp.broadcast_to(piece[None], pieces.shape))
    *dense, router, table, first_gain, second_gain = unpack_part(summed.reshape(DENSE, LANES))
    return (
        layer_out,
        grad_tokens,
        *dense,
        router.T,
        table,
        first_gain,
        second_gain,
        grad_up[None],
        grad_down[None],
    )


def solution(mesh):
    in_specs = (
        P(("expert", "wshard"), None),
        P(("expert", "wshard"), None),
        P(("expert", "wshard"), None),
        P("wshard", None),
        P("wshard", None),
        P("wshard", None),
        P("wshard", None),
        P("wshard", None),
        P("wshard", None),
        P("wshard"),
        P("wshard"),
        P("expert", None, "wshard"),
        P("expert", "wshard", None),
        P(("expert", "wshard"), None),
    )
    out_specs = (
        P(("expert", "wshard"), None),
        P(("expert", "wshard"), None),
        P("wshard", None),
        P("wshard", None),
        P("wshard", None),
        P("wshard", None),
        P("wshard", None),
        P("wshard", None),
        P("wshard"),
        P("wshard"),
        P("expert", None, "wshard"),
        P("expert", "wshard", None),
    )
    return jax.shard_map(
        per_device, mesh=mesh, in_specs=in_specs, out_specs=out_specs, check_vma=False
    )
```
